32 devices in a mesh: groups: 2 (over y), dp: 4 (over x, core), mp: 4 (over z).
Axes of the slice: x: 2, y: 2, z: 4, core: 2. Of those that a mesh axis runs over, the one named last changes fastest.
Arguments:
- activations: bfloat16 [16384, 8192], P(('groups', 'dp'), 'mp'), parts along dimension 0, may hold values from -6 to 6
- output_grads: bfloat16 [16384, 28672], P(('groups', 'dp'), 'mp'), parts along dimension 0, may hold values from -6 to 6
- grad_factors: bfloat16 [28672, 512], P('mp', 'dp'), may hold values from -0.03125 to 0.03125
- act_factors: bfloat16 [8192, 512], P('mp', 'dp'), may hold values from -0.0625 to 0.0625
Outputs:
- scores: float32 [8, 16], P(('groups', 'dp')), parts along dimension 0
The draws below stay inside these ranges and needn't reach their ends.
There are 2 independent parts, one for each index of `groups`. The reference program is written for one: setup_inputs(seed, part) draws one part's arguments, and reference() takes and returns one part's arrays. A program takes and returns all parts, laid end to end along the dimension named above; an argument that names none is the same for every part. Nothing has to cross between parts.
All inputs are finite; a program needn't handle non-finite values.
Results may differ from the reference program's by a relative error of at most 0.015.
Values may be sent and summed in bfloat16 or wider, within the bound.
A program may use at most 128 MiB of HBM per device.

```python
import jax
import jax.numpy as jnp
from jax import lax

DIN = 8192
DOUT = 28672
QUERIES = 16
RANK = 32
SEQ_LEN = 2048
COLUMNS = 512
SEQS = 4
TOKENS = 8192
N_MP = 4


def spiked(array, rng, source, target, parts, factor):
    def block_of(position):
        return (jnp.arange(array.shape[position]) // (array.shape[position] // parts)).reshape((-1,) + (1,) * (array.ndim - 1 - position))

    one_side = jax.random.permutation(rng, parts)[block_of(target)]
    second = (block_of(target) + parts // 2) % parts
    return jnp.where((block_of(source) == one_side) | (block_of(source) == second), factor * array, array)


def levels(stream_key, extent, split, least, high):
    factor_of = 1.0
    for dim, shards_of in split:
        steps = jax.random.uniform(jax.random.fold_in(jax.random.fold_in(stream_key, 6), dim), (shards_of,), jnp.float32, least / len(split), high / len(split))
        factor_of = factor_of * jnp.repeat(jnp.exp(steps), extent[dim] // shards_of).reshape((-1,) + (1,) * (len(extent) - 1 - dim))
    return factor_of


def bell_draw(rng, shape, spread, reach, split=(), kind=jnp.bfloat16):
    level = levels(rng, shape, split, -0.22, 0.18) if split else 1.0
    entries = jax.random.normal(rng, shape, jnp.float32) * spread * level
    return jnp.minimum(jnp.maximum(entries, -reach), reach).astype(kind)


def noise_with(rng, dims, spread, most, cuts, heavy, kind=jnp.bfloat16):
    entries = spread * jax.random.normal(rng, dims, jnp.float32)
    if cuts:
        entries = entries * levels(rng, dims, cuts, -0.22, 0.18)
    return jnp.clip(spiked(entries, jax.random.fold_in(rng, 3), *heavy), -most, most).astype(kind)


def setup_inputs(seed: int = 0, part: int = 0) -> dict:
    key_of = jax.random.split(jax.random.key(seed), 5)
    part_splits = jax.random.split(jax.random.fold_in(key_of[4], part), 5)
    return {
        "activations": bell_draw(part_splits[0], (TOKENS, DIN), 1.0, 6.0, ((0, 4), (1, 4))),
        "output_grads": noise_with(part_splits[1], (TOKENS, DOUT), 1.0, 6.0, ((0, 4), (1, 4)), (1, 0, 4, 2.0)),
        "grad_factors": bell_draw(key_of[2], (DOUT, COLUMNS), DOUT ** -0.5, 0.03125, ((0, 4), (1, 4))),
        "act_factors": bell_draw(key_of[3], (DIN, COLUMNS), DIN ** -0.5, 0.0625, ((0, 4), (1, 4))),
    }


def blocked_product(left, right, blocks):
    width = left.shape[1] // blocks

    def step(total, index):
        start = (index * width).astype(jnp.int32)
        part_left = lax.dynamic_slice_in_dim(left, start, width, 1)
        part_right = lax.dynamic_slice_in_dim(right, start, width, 0)
        term = jnp.dot(part_left, part_right, preferred_element_type=jnp.float32)
        return (total + term.astype(jnp.bfloat16).astype(jnp.float32), None)
    first = jnp.zeros((left.shape[0], right.shape[1]), jnp.float32)
    total, unused = lax.scan(step, first, jnp.arange(blocks, dtype=jnp.int32))
    return total

def reference(activations, output_grads, grad_factors, act_factors):
    grad_proj = blocked_product(output_grads, grad_factors, N_MP)
    act_proj = blocked_product(activations, act_factors, N_MP)
    token_scores = (grad_proj * act_proj).reshape(TOKENS, QUERIES, RANK).sum(axis=2)
    totals = token_scores.reshape(SEQS, SEQ_LEN, QUERIES).sum(axis=1)
    return totals / jnp.sqrt(jnp.float32(SEQ_LEN * RANK))
```

```python
import functools

import jax
import jax.numpy as jnp
from jax import lax
from jax.experimental import pallas as pl
from jax.experimental.pallas import tpu as pltpu
from jax.sharding import PartitionSpec as P

QUERIES = 16
RANK = 32
SEQ_LEN = 2048
SEQ_DEV = 1

BLOCKS = 8
PIECES = 7
OG_SLOTS = 3
MESH = pl.DeviceIdType.MESH


def plain_body(activations, output_grads, grad_factors, act_factors):
    full_grad, full_act = (
        lax.all_gather(grad_factors, "dp", axis=1, tiled=True),
        lax.all_gather(act_factors, "dp", axis=1, tiled=True),
    )
    tok_rows = activations.shape[0]
    columns = full_grad.shape[1]
    parts = lax.axis_size("mp")
    position = lax.axis_index("mp")
    seq_ids = jnp.arange(SEQ_DEV, dtype=jnp.int32)
    owned = tok_rows // parts
    grad_term = jnp.dot(output_grads, full_grad, preferred_element_type=jnp.float32)
    act_term = jnp.dot(activations, full_act, preferred_element_type=jnp.float32)
    summed = lax.psum_scatter(
        jnp.concatenate([grad_term, act_term], axis=1).astype(jnp.bfloat16),
        "mp",
        scatter_dimension=0,
        tiled=True,
    ).astype(jnp.float32)
    product = summed[:, :columns] * summed[:, columns:]
    token_scores = product.reshape(owned, QUERIES, RANK).sum(axis=2)
    row_seq = (position * owned + jnp.arange(owned, dtype=jnp.int32)) // SEQ_LEN
    member = (seq_ids[:, None] == row_seq[None, :]).astype(jnp.float32)
    partial_value = jnp.dot(member, token_scores, precision=lax.Precision.HIGHEST)
    totals = lax.psum(partial_value, "mp")
    return totals / jnp.sqrt(jnp.float32(SEQ_LEN * RANK))


def kernel(
    n,
    act, og, gf, af, out,
    act_v, og_v, fa, fg, own_a, g_v, tmp, acc, gath,
    p_send, p_recv, s_send, s_recv,
    load_act, load_f, load_og,
    sib_s, sib_r, xs, xr, ys, yr, sxs, sxr, sys_, syr,
    pss, prs, sss, srs, fs, fr,
):
    g = lax.axis_index("groups")
    d = lax.axis_index("dp")
    z = lax.axis_index("mp")
    core = lax.rem(d, 2)
    x = d // 2
    sib = (g, d + 1 - 2 * core, z)
    xn = (g, lax.rem(d + 2, 4), z)
    yn = (1 - g, d, z)
    rows = act.shape[0] // BLOCKS
    w = gf.shape[1]
    ka, kg = af.shape[0] // 2, gf.shape[0] // 2
    kp = kg // PIECES
    chunks = 2 * BLOCKS
    cols = pl.ds(pl.multiple_of(core * w, w), w)

    def act_load(b):
        r = pl.ds(pl.multiple_of(b * rows, rows), rows)
        return pltpu.make_async_copy(act.at[r], act_v.at[r], load_act.at[b])

    def og_load(j):
        r = pl.ds(pl.multiple_of(lax.rem(j, BLOCKS) * rows, rows), rows)
        slot = lax.rem(j, OG_SLOTS)
        return pltpu.make_async_copy(og.at[r], og_v.at[slot], load_og.at[slot])

    def remote(src, dst, ss, rs, dev):
        return pltpu.make_async_remote_copy(
            src_ref=src, dst_ref=dst, send_sem=ss, recv_sem=rs,
            device_id=dev, device_id_type=MESH,
        )

    def arows(side):
        return pl.ds(pl.multiple_of(side * ka, ka), ka)

    def grows(side, k):
        return pl.ds(pl.multiple_of(side * kg + k * kp, kp), kp)

    load_fa = pltpu.make_async_copy(af, fa.at[0, :, cols], load_f.at[0])
    load_fg = pltpu.make_async_copy(gf, fg.at[0, :, cols], load_f.at[1])
    sib_a = remote(af, fa.at[0, :, cols], sib_s.at[0], sib_r.at[0], sib)
    sib_g = remote(gf, fg.at[0, :, cols], sib_s.at[1], sib_r.at[1], sib)

    def x_a():
        return remote(af.at[arows(g)], fa.at[1, arows(g), cols], xs.at[0], xr.at[0], xn)

    def x_g(k):
        return remote(gf.at[grows(g, k)], fg.at[1, grows(g, k), cols], xs.at[k + 1], xr.at[k + 1], xn)

    def fwd_a(side, ss, rs, dev):
        ref = fa.at[1, arows(side), cols]
        return remote(ref, ref, ss.at[0], rs.at[0], dev)

    def fwd_g(side, k, ss, rs, dev):
        ref = fg.at[1, grows(side, k), cols]
        return remote(ref, ref, ss.at[k + 1], rs.at[k + 1], dev)

    load_fa.start()
    for b in range(BLOCKS):
        act_load(b).start()
    load_fg.start()
    for j in range(OG_SLOTS):
        og_load(j).start()
    acc[...] = jnp.zeros_like(acc)

    barrier = pltpu.get_barrier_semaphore()
    for dev in (sib, xn, yn):
        pl.semaphore_signal(barrier, inc=1, device_id=dev, device_id_type=MESH)
    for o in range(1, n):
        pl.semaphore_signal(
            barrier, inc=1, device_id=(g, d, lax.rem(z + o, n)), device_id_type=MESH
        )
    pl.semaphore_wait(barrier, 3 + n - 1)

    sib_a.start()
    x_a().start()
    for k in range(PIECES):
        x_g(k).start()
    sib_g.start()
    load_fa.wait()
    sib_a.wait_recv()

    def p_copy(c):
        return remote(p_send.at[c], p_recv.at[c], pss.at[c], prs.at[c], (g, d, lax.rem(z + 1, n)))

    def s_copy(c):
        return remote(s_send.at[c], s_recv.at[c], sss.at[c], srs.at[c], (g, d, lax.rem(z + n - 1, n)))

    def relay(c, first, last, copy, send, recv):
        @pl.when((c >= 0) & (c < chunks))
        def _():
            @pl.when(jnp.logical_not(first))
            def _():
                copy(c).wait_recv()

                @pl.when(jnp.logical_not(last))
                def _():
                    send[c] = (own_a[c] + recv[c].astype(jnp.float32)).astype(jnp.bfloat16)

            @pl.when(first)
            def _():
                send[c] = own_a[c].astype(jnp.bfloat16)

            @pl.when(jnp.logical_not(last))
            def _():
                copy(c).start()

    h1_step = 12

    def step(s, carry):
        @pl.when(s < BLOCKS)
        def _():
            act_load(s).wait()

        @pl.when(s == BLOCKS)
        def _():
            fwd_a(g, sxs, sxr, sib).wait_recv()
            fwd_a(1 - g, sys_, syr, sib).wait_recv()

        @pl.when(s < chunks)
        def _():
            b = lax.rem(s, BLOCKS)
            r = pl.ds(pl.multiple_of(b * rows, rows), rows)
            own_a[s] = jnp.dot(
                act_v[r, :], fa[s // BLOCKS], preferred_element_type=jnp.float32
            )

        relay(s - z, z == 0, z == n - 1, p_copy, p_send, p_recv)
        relay(s - (n - 1 - z), z == n - 1, z == 0, s_copy, s_send, s_recv)

        @pl.when(s == 2)
        def _():
            x_a().wait_recv()
            fwd_a(g, ys, yr, yn).start()
            fwd_a(g, sxs, sxr, sib).start()

        @pl.when((s >= 3) & (s < 3 + PIECES))
        def _():
            k = s - 3
            x_g(k).wait_recv()
            fwd_g(g, k, ys, yr, yn).start()
            fwd_g(g, k, sxs, sxr, sib).start()

        @pl.when(s == 4)
        def _():
            fwd_a(1 - g, ys, yr, yn).wait_recv()
            fwd_a(1 - g, sys_, syr, sib).start()

        @pl.when((s >= 5) & (s < 5 + PIECES))
        def _():
            k = s - 5
            fwd_g(1 - g, k, ys, yr, yn).wait_recv()
            fwd_g(1 - g, k, sys_, syr, sib).start()

        @pl.when(s == 2)
        def _():
            load_fg.wait()
            sib_g.wait_recv()

        @pl.when(s == h1_step)
        def _():
            def got(k, carry):
                fwd_g(g, k, sxs, sxr, sib).wait_recv()
                fwd_g(1 - g, k, sys_, syr, sib).wait_recv()
                return carry

            lax.fori_loop(0, PIECES, got, 0)

        early = (s >= 2) & (s < 2 + BLOCKS)
        late = (s >= h1_step) & (s < h1_step + BLOCKS // 2)
        first = jnp.where(early, s - 2, BLOCKS + 2 * (s - h1_step))
        count = jnp.where(early, 1, jnp.where(late, 2, 0))

        def grad_block(i, carry):
            j = first + i
            og_load(j).wait()
            g_v[j] = jnp.dot(
                og_v[lax.rem(j, OG_SLOTS)], fg[j // BLOCKS],
                preferred_element_type=jnp.float32,
            )

            @pl.when(j + OG_SLOTS < chunks)
            def _():
                og_load(j + OG_SLOTS).start()

            return carry

        lax.fori_loop(0, count, grad_block, 0)

        c = s - n

        @pl.when(c >= 0)
        def _():
            tmp[...] = own_a[c]

            @pl.when(z > 0)
            def _():
                tmp[...] += p_recv[c].astype(jnp.float32)

            @pl.when(z < n - 1)
            def _():
                tmp[...] += s_recv[c].astype(jnp.float32)

            prod = (tmp[...] * g_v[c]).reshape(rows // 8, 8, 2 * w).sum(axis=0)
            half = c // BLOCKS
            place = half + x - 2 * half * x
            at = pl.ds(pl.multiple_of(place * 2 * w, 2 * w), 2 * w)
            acc[:, at] += prod

        return carry

    lax.fori_loop(0, chunks + n, step, 0)

    gath[z] = acc[...]

    def final(o):
        return remote(acc, gath.at[z], fs.at[o], fr.at[o], (g, d, lax.rem(z + o, n)))

    def final_in(o):
        src = lax.rem(z + n - o, n)
        return remote(acc, gath.at[src], fs.at[o], fr.at[o], (g, d, src))

    for o in range(1, n):
        final(o).start()

    sib_a.wait_send()
    sib_g.wait_send()
    x_a().wait_send()
    fwd_a(g, ys, yr, yn).wait_send()
    fwd_a(g, sxs, sxr, sib).wait_send()
    fwd_a(1 - g, sys_, syr, sib).wait_send()

    def sent(k, carry):
        x_g(k).wait_send()
        fwd_g(g, k, ys, yr, yn).wait_send()
        fwd_g(g, k, sxs, sxr, sib).wait_send()
        fwd_g(1 - g, k, sys_, syr, sib).wait_send()
        return carry

    lax.fori_loop(0, PIECES, sent, 0)

    @pl.when(z < n - 1)
    def _():
        def sent_p(c, carry):
            p_copy(c).wait_send()
            return carry

        lax.fori_loop(0, chunks, sent_p, 0)

    @pl.when(z > 0)
    def _():
        def sent_s(c, carry):
            s_copy(c).wait_send()
            return carry

        lax.fori_loop(0, chunks, sent_s, 0)

    for o in range(1, n):
        final_in(o).wait_recv()
    for o in range(1, n):
        final(o).wait_send()
    total = gath[0]
    for i in range(1, n):
        total = total + gath[i]
    out[...] = total


def kernel_body(n, activations, output_grads, grad_factors, act_factors):
    tokens, ka = activations.shape
    kg, w = grad_factors.shape
    rows = tokens // BLOCKS
    chunks = 2 * BLOCKS
    bf, f32 = jnp.bfloat16, jnp.float32
    dma = pltpu.SemaphoreType.DMA
    block = (chunks, rows, 2 * w)
    total = pl.pallas_call(
        functools.partial(kernel, n),
        out_shape=jax.ShapeDtypeStruct((8, 4 * w), f32),
        in_specs=[pl.BlockSpec(memory_space=pl.ANY)] * 4,
        out_specs=pl.BlockSpec(memory_space=pltpu.VMEM),
        scratch_shapes=[
            pltpu.VMEM((tokens, ka), bf),
            pltpu.VMEM((OG_SLOTS, rows, kg), bf),
            pltpu.VMEM((2, ka, 2 * w), bf),
            pltpu.VMEM((2, kg, 2 * w), bf),
            pltpu.VMEM(block, f32),
            pltpu.VMEM(block, f32),
            pltpu.VMEM((rows, 2 * w), f32),
            pltpu.VMEM((8, 4 * w), f32),
            pltpu.VMEM((n, 8, 4 * w), f32),
        ]
        + [pltpu.VMEM(block, bf)] * 4
        + [dma((BLOCKS,)), dma((2,)), dma((OG_SLOTS,)), dma((2,)), dma((2,))]
        + [dma((PIECES + 1,))] * 8
        + [dma((chunks,))] * 4
        + [dma((n,))] * 2,
        compiler_params=pltpu.CompilerParams(
            collective_id=0, has_side_effects=True, vmem_limit_bytes=58 * 2**20
        ),
        cost_estimate=pl.CostEstimate(
            flops=2 * tokens * (ka + kg) * 4 * w,
            bytes_accessed=2 * tokens * (ka + 2 * kg),
            transcendentals=0,
        ),
    )(activations, output_grads, grad_factors, act_factors)
    scores = total.sum(axis=0).reshape(QUERIES, RANK).sum(axis=1)
    return scores[None, :] / jnp.sqrt(jnp.float32(SEQ_LEN * RANK))


def solution(mesh):
    shape = dict(mesh.shape)

    def body(activations, output_grads, grad_factors, act_factors):
        kg, w = grad_factors.shape
        fits = (
            shape["groups"] == 2
            and shape["dp"] == 4
            and 4 <= shape["mp"] <= 7
            and w == 128
            and activations.shape[0] == SEQ_LEN
            and activations.shape[1] % 32 == 0
            and kg % (32 * PIECES) == 0
        )
        run = functools.partial(kernel_body, shape["mp"]) if fits else plain_body
        return run(activations, output_grads, grad_factors, act_factors)

    return jax.shard_map(
        body,
        mesh=mesh,
        in_specs=(
            P(("groups", "dp"), "mp"),
            P(("groups", "dp"), "mp"),
            P("mp", "dp"),
            P("mp", "dp"),
        ),
        out_specs=P(("groups", "dp"), None),
        check_vma=False,
    )
```

```python
import functools

import jax
import jax.numpy as jnp
from jax import lax
from jax.experimental import pallas as pl
from jax.experimental.pallas import tpu as pltpu
from jax.sharding import PartitionSpec as P

QUERIES = 16
RANK = 32
SEQ_LEN = 2048
SEQ_DEV = 1

BLOCKS = 8
SUB = 2
SKEW = 3
GROUP = 1
PIECES = 14
OG_SLOTS = 3
X_FIRST, Y_FIRST, X_EVERY = 3, 7, 1
MESH = pl.DeviceIdType.MESH


def plain_body(activations, output_grads, grad_factors, act_factors):
    full_grad, full_act = (
        lax.all_gather(grad_factors, "dp", axis=1, tiled=True),
        lax.all_gather(act_factors, "dp", axis=1, tiled=True),
    )
    tok_rows = activations.shape[0]
    columns = full_grad.shape[1]
    parts = lax.axis_size("mp")
    position = lax.axis_index("mp")
    seq_ids = jnp.arange(SEQ_DEV, dtype=jnp.int32)
    owned = tok_rows // parts
    grad_term = jnp.dot(output_grads, full_grad, preferred_element_type=jnp.float32)
    act_term = jnp.dot(activations, full_act, preferred_element_type=jnp.float32)
    summed = lax.psum_scatter(
        jnp.concatenate([grad_term, act_term], axis=1).astype(jnp.bfloat16),
        "mp",
        scatter_dimension=0,
        tiled=True,
    ).astype(jnp.float32)
    product = summed[:, :columns] * summed[:, columns:]
    token_scores = product.reshape(owned, QUERIES, RANK).sum(axis=2)
    row_seq = (position * owned + jnp.arange(owned, dtype=jnp.int32)) // SEQ_LEN
    member = (seq_ids[:, None] == row_seq[None, :]).astype(jnp.float32)
    partial_value = jnp.dot(member, token_scores, precision=lax.Precision.HIGHEST)
    totals = lax.psum(partial_value, "mp")
    return totals / jnp.sqrt(jnp.float32(SEQ_LEN * RANK))


def kernel(
    n,
    act, og, gf, af, out,
    act_v, og_v, fa, fg, own_a, g_v, tmp, acc, gath,
    p_send, p_recv, s_send, s_recv,
    load_act, load_f, load_og,
    sib_s, sib_r, xs, xr, ys, yr, sxs, sxr, sys_, syr,
    pss, prs, sss, srs, fs, fr,
):
    g = lax.axis_index("groups")
    d = lax.axis_index("dp")
    z = lax.axis_index("mp")
    core = lax.rem(d, 2)
    x = d // 2
    sib = (g, d + 1 - 2 * core, z)
    xn = (g, lax.rem(d + 2, 4), z)
    yn = (1 - g, d, z)
    rows = act.shape[0] // BLOCKS
    w = gf.shape[1]
    ka, kg = af.shape[0] // 2, gf.shape[0] // 2
    kp = kg // PIECES
    sub = rows // SUB
    chunks = 2 * BLOCKS * SUB
    lag = SKEW * (n - 1) + 1
    per = SUB * GROUP
    gblocks = BLOCKS // GROUP
    cols = pl.ds(pl.multiple_of(core * w, w), w)

    def act_load(b):
        r = pl.ds(pl.multiple_of(b * rows, rows), rows)
        return pltpu.make_async_copy(act.at[r], act_v.at[r], load_act.at[b])

    def og_load(j):
        m = rows * GROUP
        r = pl.ds(pl.multiple_of(lax.rem(j, gblocks) * m, m), m)
        slot = lax.rem(j, OG_SLOTS)
        return pltpu.make_async_copy(og.at[r], og_v.at[slot], load_og.at[slot])

    def remote(src, dst, ss, rs, dev):
        return pltpu.make_async_remote_copy(
            src_ref=src, dst_ref=dst, send_sem=ss, recv_sem=rs,
            device_id=dev, device_id_type=MESH,
        )

    def arows(side):
        return pl.ds(pl.multiple_of(side * ka, ka), ka)

    def grows(side, k):
        return pl.ds(pl.multiple_of(side * kg + k * kp, kp), kp)

    load_fa = pltpu.make_async_copy(af, fa.at[0, :, cols], load_f.at[0])
    load_fg = pltpu.make_async_copy(gf, fg.at[0, :, cols], load_f.at[1])
    sib_a = remote(af, fa.at[0, :, cols], sib_s.at[0], sib_r.at[0], sib)
    sib_g = remote(gf, fg.at[0, :, cols], sib_s.at[1], sib_r.at[1], sib)

    def x_a():
        return remote(af.at[arows(g)], fa.at[1, arows(g), cols], xs.at[0], xr.at[0], xn)

    def x_g(k):
        return remote(gf.at[grows(g, k)], fg.at[1, grows(g, k), cols], xs.at[k + 1], xr.at[k + 1], xn)

    def fwd_a(side, ss, rs, dev):
        ref = fa.at[1, arows(side), cols]
        return remote(ref, ref, ss.at[0], rs.at[0], dev)

    def fwd_g(side, k, ss, rs, dev):
        ref = fg.at[1, grows(side, k), cols]
        return remote(ref, ref, ss.at[k + 1], rs.at[k + 1], dev)

    load_fa.start()
    act_load(0).start()
    acc[...] = jnp.zeros_like(acc)

    barrier = pltpu.get_barrier_semaphore()
    for dev in (sib, xn, yn):
        pl.semaphore_signal(barrier, inc=1, device_id=dev, device_id_type=MESH)
    for o in range(1, n):
        pl.semaphore_signal(
            barrier, inc=1, device_id=(g, d, lax.rem(z + o, n)), device_id_type=MESH
        )
    pl.semaphore_wait(barrier, 3 + n - 1)

    sib_a.start()
    x_a().start()
    for k in range(PIECES):
        x_g(k).start()
    sib_g.start()
    for b in range(1, BLOCKS):
        act_load(b).start()
    load_fa.wait()
    sib_a.wait_recv()

    def p_copy(c):
        return remote(p_send.at[c], p_recv.at[c], pss.at[c], prs.at[c], (g, d, lax.rem(z + 1, n)))

    def s_copy(c):
        return remote(s_send.at[c], s_recv.at[c], sss.at[c], srs.at[c], (g, d, lax.rem(z + n - 1, n)))

    def relay(c, first, last, copy, send, recv):
        @pl.when((c >= 0) & (c < chunks))
        def _():
            @pl.when(jnp.logical_not(first))
            def _():
                copy(c).wait_recv()

                @pl.when(jnp.logical_not(last))
                def _():
                    send[c] = (own_a[c] + recv[c].astype(jnp.float32)).astype(jnp.bfloat16)

            @pl.when(first)
            def _():
                send[c] = own_a[c].astype(jnp.bfloat16)

            @pl.when(jnp.logical_not(last))
            def _():
                copy(c).start()

    def step(s, carry):
        b = s // SUB
        block_start = lax.rem(s, SUB) == 0

        @pl.when(block_start & (b < BLOCKS))
        def _():
            act_load(b).wait()

        @pl.when(s == BLOCKS * SUB)
        def _():
            fwd_a(g, sxs, sxr, sib).wait_recv()
            fwd_a(1 - g, sys_, syr, sib).wait_recv()

        @pl.when(block_start & (s < chunks))
        def _():
            r = pl.ds(pl.multiple_of(lax.rem(b, BLOCKS) * rows, rows), rows)
            own_a[pl.ds(pl.multiple_of(b * SUB, SUB), SUB)] = jnp.dot(
                act_v[r, :], fa[b // BLOCKS], preferred_element_type=jnp.float32
            ).reshape(SUB, sub, 2 * w)

        relay(s - SKEW * z, z == 0, z == n - 1, p_copy, p_send, p_recv)
        relay(s - SKEW * (n - 1 - z), z == n - 1, z == 0, s_copy, s_send, s_recv)

        @pl.when(s == 2)
        def _():
            load_fg.start()
            for j in range(OG_SLOTS):
                og_load(j).start()

        @pl.when(s == X_FIRST)
        def _():
            x_a().wait_recv()
            fwd_a(g, ys, yr, yn).start()
            fwd_a(g, sxs, sxr, sib).start()

        u = s - (X_FIRST + X_EVERY)

        @pl.when((u >= 0) & (u < X_EVERY * PIECES) & (lax.rem(s + X_EVERY * X_FIRST - X_FIRST, X_EVERY) == 0))
        def _():
            k = u // X_EVERY
            x_g(k).wait_recv()
            fwd_g(g, k, ys, yr, yn).start()
            fwd_g(g, k, sxs, sxr, sib).start()

        @pl.when(s == Y_FIRST)
        def _():
            fwd_a(1 - g, ys, yr, yn).wait_recv()
            fwd_a(1 - g, sys_, syr, sib).start()

        v = s - (Y_FIRST + X_EVERY)

        @pl.when((v >= 0) & (v < X_EVERY * PIECES) & (lax.rem(s + X_EVERY * Y_FIRST - Y_FIRST, X_EVERY) == 0))
        def _():
            k = v // X_EVERY
            fwd_g(1 - g, k, ys, yr, yn).wait_recv()
            fwd_g(1 - g, k, sys_, syr, sib).start()

        c = s - lag

        @pl.when(c == 0)
        def _():
            load_fg.wait()
            sib_g.wait_recv()

        @pl.when(c == BLOCKS * SUB)
        def _():
            def got(k, carry):
                fwd_g(g, k, sxs, sxr, sib).wait_recv()
                fwd_g(1 - g, k, sys_, syr, sib).wait_recv()
                return carry

            lax.fori_loop(0, PIECES, got, 0)

        @pl.when((c >= 0) & (lax.rem(s + per * lag - lag, per) == 0))
        def _():
            j = c // per
            og_load(j).wait()
            g_v[...] = jnp.dot(
                og_v[lax.rem(j, OG_SLOTS)], fg[j // gblocks],
                preferred_element_type=jnp.float32,
            ).reshape(per, sub, 2 * w)

            @pl.when(j + OG_SLOTS < 2 * gblocks)
            def _():
                og_load(j + OG_SLOTS).start()

        @pl.when(c >= 0)
        def _():
            tmp[...] = own_a[c]

            @pl.when(z > 0)
            def _():
                tmp[...] += p_recv[c].astype(jnp.float32)

            @pl.when(z < n - 1)
            def _():
                tmp[...] += s_recv[c].astype(jnp.float32)

            prod = (tmp[...] * g_v[lax.rem(c, per)]).reshape(sub // 8, 8, 2 * w).sum(axis=0)
            half = c // (BLOCKS * SUB)
            place = half + x - 2 * half * x
            at = pl.ds(pl.multiple_of(place * 2 * w, 2 * w), 2 * w)
            acc[:, at] += prod

        return carry

    lax.fori_loop(0, chunks + lag, step, 0)

    gath[z] = acc[...]

    def final(o):
        return remote(acc, gath.at[z], fs.at[o], fr.at[o], (g, d, lax.rem(z + o, n)))

    def final_in(o):
        src = lax.rem(z + n - o, n)
        return remote(acc, gath.at[src], fs.at[o], fr.at[o], (g, d, src))

    for o in range(1, n):
        final(o).start()

    sib_a.wait_send()
    sib_g.wait_send()
    x_a().wait_send()
    fwd_a(g, ys, yr, yn).wait_send()
    fwd_a(g, sxs, sxr, sib).wait_send()
    fwd_a(1 - g, sys_, syr, sib).wait_send()

    def sent(k, carry):
        x_g(k).wait_send()
        fwd_g(g, k, ys, yr, yn).wait_send()
        fwd_g(g, k, sxs, sxr, sib).wait_send()
        fwd_g(1 - g, k, sys_, syr, sib).wait_send()
        return carry

    lax.fori_loop(0, PIECES, sent, 0)

    @pl.when(z < n - 1)
    def _():
        def sent_p(c, carry):
            p_copy(c).wait_send()
            return carry

        lax.fori_loop(0, chunks, sent_p, 0)

    @pl.when(z > 0)
    def _():
        def sent_s(c, carry):
            s_copy(c).wait_send()
            return carry

        lax.fori_loop(0, chunks, sent_s, 0)

    for o in range(1, n):
        final_in(o).wait_recv()
    for o in range(1, n):
        final(o).wait_send()
    total = gath[0]
    for i in range(1, n):
        total = total + gath[i]
    out[...] = total


def kernel_body(n, activations, output_grads, grad_factors, act_factors):
    tokens, ka = activations.shape
    kg, w = grad_factors.shape
    rows = tokens // BLOCKS
    chunks = 2 * BLOCKS * SUB
    bf, f32 = jnp.bfloat16, jnp.float32
    dma = pltpu.SemaphoreType.DMA
    block = (chunks, rows // SUB, 2 * w)
    total = pl.pallas_call(
        functools.partial(kernel, n),
        out_shape=jax.ShapeDtypeStruct((8, 4 * w), f32),
        in_specs=[pl.BlockSpec(memory_space=pl.ANY)] * 4,
        out_specs=pl.BlockSpec(memory_space=pltpu.VMEM),
        scratch_shapes=[
            pltpu.VMEM((tokens, ka), bf),
            pltpu.VMEM((OG_SLOTS, GROUP * rows, kg), bf),
            pltpu.VMEM((2, ka, 2 * w), bf),
            pltpu.VMEM((2, kg, 2 * w), bf),
            pltpu.VMEM(block, f32),
            pltpu.VMEM((SUB * GROUP,) + block[1:], f32),
            pltpu.VMEM(block[1:], f32),
            pltpu.VMEM((8, 4 * w), f32),
            pltpu.VMEM((n, 8, 4 * w), f32),
        ]
        + [pltpu.VMEM(block, bf)] * 4
        + [dma((BLOCKS,)), dma((2,)), dma((OG_SLOTS,)), dma((2,)), dma((2,))]
        + [dma((PIECES + 1,))] * 8
        + [dma((chunks,))] * 4
        + [dma((n,))] * 2,
        compiler_params=pltpu.CompilerParams(
            collective_id=0, has_side_effects=True, vmem_limit_bytes=58 * 2**20
        ),
        cost_estimate=pl.CostEstimate(
            flops=2 * tokens * (ka + kg) * 4 * w,
            bytes_accessed=2 * tokens * (ka + 2 * kg),
            transcendentals=0,
        ),
    )(activations, output_grads, grad_factors, act_factors)
    scores = total.sum(axis=0).reshape(QUERIES, RANK).sum(axis=1)
    return scores[None, :] / jnp.sqrt(jnp.float32(SEQ_LEN * RANK))


def solution(mesh):
    shape = dict(mesh.shape)

    def body(activations, output_grads, grad_factors, act_factors):
        kg, w = grad_factors.shape
        fits = (
            shape["groups"] == 2
            and shape["dp"] == 4
            and 4 <= shape["mp"] <= 7
            and w == 128
            and activations.shape[0] == SEQ_LEN
            and activations.shape[1] % 32 == 0
            and kg % (32 * PIECES) == 0
        )
        run = functools.partial(kernel_body, shape["mp"]) if fits else plain_body
        return run(activations, output_grads, grad_factors, act_factors)

    return jax.shard_map(
        body,
        mesh=mesh,
        in_specs=(
            P(("groups", "dp"), "mp"),
            P(("groups", "dp"), "mp"),
            P("mp", "dp"),
            P("mp", "dp"),
        ),
        out_specs=P(("groups", "dp"), None),
        check_vma=False,
    )
```

```python
import functools

import jax
import jax.numpy as jnp
from jax import lax
from jax.experimental import pallas as pl
from jax.experimental.pallas import tpu as pltpu
from jax.sharding import PartitionSpec as P

QUERIES = 16
RANK = 32
SEQ_LEN = 2048
SEQ_DEV = 1

BLOCKS = 8
SUB = 2
SKEW = 3
GROUP = 1
PIECES = 14
OG_SLOTS = 3
X_FIRST, Y_FIRST, X_EVERY = 5, 9, 1
MESH = pl.DeviceIdType.MESH


def plain_body(activations, output_grads, grad_factors, act_factors):
    full_grad, full_act = (
        lax.all_gather(grad_factors, "dp", axis=1, tiled=True),
        lax.all_gather(act_factors, "dp", axis=1, tiled=True),
    )
    tok_rows = activations.shape[0]
    columns = full_grad.shape[1]
    parts = lax.axis_size("mp")
    position = lax.axis_index("mp")
    seq_ids = jnp.arange(SEQ_DEV, dtype=jnp.int32)
    owned = tok_rows // parts
    grad_term = jnp.dot(output_grads, full_grad, preferred_element_type=jnp.float32)
    act_term = jnp.dot(activations, full_act, preferred_element_type=jnp.float32)
    summed = lax.psum_scatter(
        jnp.concatenate([grad_term, act_term], axis=1).astype(jnp.bfloat16),
        "mp",
        scatter_dimension=0,
        tiled=True,
    ).astype(jnp.float32)
    product = summed[:, :columns] * summed[:, columns:]
    token_scores = product.reshape(owned, QUERIES, RANK).sum(axis=2)
    row_seq = (position * owned + jnp.arange(owned, dtype=jnp.int32)) // SEQ_LEN
    member = (seq_ids[:, None] == row_seq[None, :]).astype(jnp.float32)
    partial_value = jnp.dot(member, token_scores, precision=lax.Precision.HIGHEST)
    totals = lax.psum(partial_value, "mp")
    return totals / jnp.sqrt(jnp.float32(SEQ_LEN * RANK))


def kernel(
    n,
    act, og, gf, af, out,
    act_v, og_v, fa, fg, own_a, g_v, tmp, acc, gath,
    p_send, p_recv, s_send, s_recv,
    load_act, load_f, load_og,
    sib_s, sib_r, xs, xr, ys, yr, sxs, sxr, sys_, syr,
    pss, prs, sss, srs, fs, fr,
):
    g = lax.axis_index("groups")
    d = lax.axis_index("dp")
    z = lax.axis_index("mp")
    core = lax.rem(d, 2)
    x = d // 2
    sib = (g, d + 1 - 2 * core, z)
    xn = (g, lax.rem(d + 2, 4), z)
    yn = (1 - g, d, z)
    rows = act.shape[0] // BLOCKS
    w = gf.shape[1]
    ka, kg = af.shape[0] // 2, gf.shape[0] // 2
    kp = kg // PIECES
    sub = rows // SUB
    chunks = 2 * BLOCKS * SUB
    lag = SKEW * (n - 1) + 1
    per = SUB * GROUP
    gblocks = BLOCKS // GROUP
    cols = pl.ds(pl.multiple_of(core * w, w), w)

    def act_load(b):
        r = pl.ds(pl.multiple_of(b * rows, rows), rows)
        return pltpu.make_async_copy(act.at[r], act_v.at[r], load_act.at[b])

    def og_load(j):
        m = rows * GROUP
        r = pl.ds(pl.multiple_of(lax.rem(j, gblocks) * m, m), m)
        slot = lax.rem(j, OG_SLOTS)
        return pltpu.make_async_copy(og.at[r], og_v.at[slot], load_og.at[slot])

    def remote(src, dst, ss, rs, dev):
        return pltpu.make_async_remote_copy(
            src_ref=src, dst_ref=dst, send_sem=ss, recv_sem=rs,
            device_id=dev, device_id_type=MESH,
        )

    def arows(side):
        return pl.ds(pl.multiple_of(side * ka, ka), ka)

    def grows(side, k):
        return pl.ds(pl.multiple_of(side * kg + k * kp, kp), kp)

    load_fa = pltpu.make_async_copy(af, fa.at[0, :, cols], load_f.at[0])
    load_fg = pltpu.make_async_copy(gf, fg.at[0, :, cols], load_f.at[1])
    sib_a = remote(af, fa.at[0, :, cols], sib_s.at[0], sib_r.at[0], sib)
    sib_g = remote(gf, fg.at[0, :, cols], sib_s.at[1], sib_r.at[1], sib)

    def x_a():
        return remote(af.at[arows(g)], fa.at[1, arows(g), cols], xs.at[0], xr.at[0], xn)

    def x_g(k):
        return remote(gf.at[grows(g, k)], fg.at[1, grows(g, k), cols], xs.at[k + 1], xr.at[k + 1], xn)

    def fwd_a(side, ss, rs, dev):
        ref = fa.at[1, arows(side), cols]
        return remote(ref, ref, ss.at[0], rs.at[0], dev)

    def fwd_g(side, k, ss, rs, dev):
        ref = fg.at[1, grows(side, k), cols]
        return remote(ref, ref, ss.at[k + 1], rs.at[k + 1], dev)

    load_fa.start()
    act_load(0).start()
    acc[...] = jnp.zeros_like(acc)

    barrier = pltpu.get_barrier_semaphore()
    for dev in (sib, xn, yn):
        pl.semaphore_signal(barrier, inc=1, device_id=dev, device_id_type=MESH)
    for o in range(1, n):
        pl.semaphore_signal(
            barrier, inc=1, device_id=(g, d, lax.rem(z + o, n)), device_id_type=MESH
        )
    pl.semaphore_wait(barrier, 3 + n - 1)

    sib_a.start()
    x_a().start()
    for k in range(PIECES):
        x_g(k).start()
    sib_g.start()
    for b in range(1, BLOCKS):
        act_load(b).start()
    load_fa.wait()
    sib_a.wait_recv()

    def p_copy(c):
        return remote(p_send.at[c], p_recv.at[c], pss.at[c], prs.at[c], (g, d, lax.rem(z + 1, n)))

    def s_copy(c):
        return remote(s_send.at[c], s_recv.at[c], sss.at[c], srs.at[c], (g, d, lax.rem(z + n - 1, n)))

    def relay(c, first, last, copy, send, recv):
        @pl.when((c >= 0) & (c < chunks))
        def _():
            @pl.when(jnp.logical_not(first))
            def _():
                copy(c).wait_recv()

                @pl.when(jnp.logical_not(last))
                def _():
                    send[c] = (own_a[c] + recv[c].astype(jnp.float32)).astype(jnp.bfloat16)

            @pl.when(first)
            def _():
                send[c] = own_a[c].astype(jnp.bfloat16)

            @pl.when(jnp.logical_not(last))
            def _():
                copy(c).start()

    def step(s, carry):
        b = s // SUB
        block_start = lax.rem(s, SUB) == 0

        @pl.when(block_start & (b < BLOCKS))
        def _():
            act_load(b).wait()

        @pl.when(s == BLOCKS * SUB)
        def _():
            fwd_a(g, sxs, sxr, sib).wait_recv()
            fwd_a(1 - g, sys_, syr, sib).wait_recv()

        @pl.when(block_start & (s < chunks))
        def _():
            r = pl.ds(pl.multiple_of(lax.rem(b, BLOCKS) * rows, rows), rows)
            own_a[pl.ds(pl.multiple_of(b * SUB, SUB), SUB)] = jnp.dot(
                act_v[r, :], fa[b // BLOCKS], preferred_element_type=jnp.float32
            ).reshape(SUB, sub, 2 * w)

        relay(s - SKEW * z, z == 0, z == n - 1, p_copy, p_send, p_recv)
        relay(s - SKEW * (n - 1 - z), z == n - 1, z == 0, s_copy, s_send, s_recv)

        @pl.when(s == 2)
        def _():
            load_fg.start()
            for j in range(OG_SLOTS):
                og_load(j).start()

        @pl.when(s == X_FIRST)
        def _():
            x_a().wait_recv()
            fwd_a(g, ys, yr, yn).start()
            fwd_a(g, sxs, sxr, sib).start()

        u = s - (X_FIRST + X_EVERY)

        @pl.when((u >= 0) & (u < X_EVERY * PIECES) & (lax.rem(s + X_EVERY * X_FIRST - X_FIRST, X_EVERY) == 0))
        def _():
            k = u // X_EVERY
            x_g(k).wait_recv()
            fwd_g(g, k, ys, yr, yn).start()
            fwd_g(g, k, sxs, sxr, sib).start()

        @pl.when(s == Y_FIRST)
        def _():
            fwd_a(1 - g, ys, yr, yn).wait_recv()
            fwd_a(1 - g, sys_, syr, sib).start()

        v = s - (Y_FIRST + X_EVERY)

        @pl.when((v >= 0) & (v < X_EVERY * PIECES) & (lax.rem(s + X_EVERY * Y_FIRST - Y_FIRST, X_EVERY) == 0))
        def _():
            k = v // X_EVERY
            fwd_g(1 - g, k, ys, yr, yn).wait_recv()
            fwd_g(1 - g, k, sys_, syr, sib).start()

        c = s - lag

        @pl.when(c == 0)
        def _():
            load_fg.wait()
            sib_g.wait_recv()

        @pl.when(c == BLOCKS * SUB)
        def _():
            def got(k, carry):
                fwd_g(g, k, sxs, sxr, sib).wait_recv()
                fwd_g(1 - g, k, sys_, syr, sib).wait_recv()
                return carry

            lax.fori_loop(0, PIECES, got, 0)

        @pl.when((c >= 0) & (lax.rem(s + per * lag - lag, per) == 0))
        def _():
            j = c // per
            og_load(j).wait()
            g_v[...] = jnp.dot(
                og_v[lax.rem(j, OG_SLOTS)], fg[j // gblocks],
                preferred_element_type=jnp.float32,
            ).reshape(per, sub, 2 * w)

            @pl.when(j + OG_SLOTS < 2 * gblocks)
            def _():
                og_load(j + OG_SLOTS).start()

        @pl.when(c >= 0)
        def _():
            tmp[...] = own_a[c]

            @pl.when(z > 0)
            def _():
                tmp[...] += p_recv[c].astype(jnp.float32)

            @pl.when(z < n - 1)
            def _():
                tmp[...] += s_recv[c].astype(jnp.float32)

            prod = (tmp[...] * g_v[lax.rem(c, per)]).reshape(sub // 8, 8, 2 * w).sum(axis=0)
            half = c // (BLOCKS * SUB)
            place = half + x - 2 * half * x
            at = pl.ds(pl.multiple_of(place * 2 * w, 2 * w), 2 * w)
            acc[:, at] += prod

        return carry

    lax.fori_loop(0, chunks + lag, step, 0)

    gath[z] = acc[...]

    def final(o):
        return remote(acc, gath.at[z], fs.at[o], fr.at[o], (g, d, lax.rem(z + o, n)))

    def final_in(o):
        src = lax.rem(z + n - o, n)
        return remote(acc, gath.at[src], fs.at[o], fr.at[o], (g, d, src))

    for o in range(1, n):
        final(o).start()

    sib_a.wait_send()
    sib_g.wait_send()
    x_a().wait_send()
    fwd_a(g, ys, yr, yn).wait_send()
    fwd_a(g, sxs, sxr, sib).wait_send()
    fwd_a(1 - g, sys_, syr, sib).wait_send()

    def sent(k, carry):
        x_g(k).wait_send()
        fwd_g(g, k, ys, yr, yn).wait_send()
        fwd_g(g, k, sxs, sxr, sib).wait_send()
        fwd_g(1 - g, k, sys_, syr, sib).wait_send()
        return carry

    lax.fori_loop(0, PIECES, sent, 0)

    @pl.when(z < n - 1)
    def _():
        def sent_p(c, carry):
            p_copy(c).wait_send()
            return carry

        lax.fori_loop(0, chunks, sent_p, 0)

    @pl.when(z > 0)
    def _():
        def sent_s(c, carry):
            s_copy(c).wait_send()
            return carry

        lax.fori_loop(0, chunks, sent_s, 0)

    for o in range(1, n):
        final_in(o).wait_recv()
    for o in range(1, n):
        final(o).wait_send()
    total = gath[0]
    for i in range(1, n):
        total = total + gath[i]
    out[...] = total


def kernel_body(n, activations, output_grads, grad_factors, act_factors):
    tokens, ka = activations.shape
    kg, w = grad_factors.shape
    rows = tokens // BLOCKS
    chunks = 2 * BLOCKS * SUB
    bf, f32 = jnp.bfloat16, jnp.float32
    dma = pltpu.SemaphoreType.DMA
    block = (chunks, rows // SUB, 2 * w)
    total = pl.pallas_call(
        functools.partial(kernel, n),
        out_shape=jax.ShapeDtypeStruct((8, 4 * w), f32),
        in_specs=[pl.BlockSpec(memory_space=pl.ANY)] * 4,
        out_specs=pl.BlockSpec(memory_space=pltpu.VMEM),
        scratch_shapes=[
            pltpu.VMEM((tokens, ka), bf),
            pltpu.VMEM((OG_SLOTS, GROUP * rows, kg), bf),
            pltpu.VMEM((2, ka, 2 * w), bf),
            pltpu.VMEM((2, kg, 2 * w), bf),
            pltpu.VMEM(block, f32),
            pltpu.VMEM((SUB * GROUP,) + block[1:], f32),
            pltpu.VMEM(block[1:], f32),
            pltpu.VMEM((8, 4 * w), f32),
            pltpu.VMEM((n, 8, 4 * w), f32),
        ]
        + [pltpu.VMEM(block, bf)] * 4
        + [dma((BLOCKS,)), dma((2,)), dma((OG_SLOTS,)), dma((2,)), dma((2,))]
        + [dma((PIECES + 1,))] * 8
        + [dma((chunks,))] * 4
        + [dma((n,))] * 2,
        compiler_params=pltpu.CompilerParams(
            collective_id=0, has_side_effects=True, vmem_limit_bytes=58 * 2**20
        ),
        cost_estimate=pl.CostEstimate(
            flops=2 * tokens * (ka + kg) * 4 * w,
            bytes_accessed=2 * tokens * (ka + 2 * kg),
            transcendentals=0,
        ),
    )(activations, output_grads, grad_factors, act_factors)
    scores = total.sum(axis=0).reshape(QUERIES, RANK).sum(axis=1)
    return scores[None, :] / jnp.sqrt(jnp.float32(SEQ_LEN * RANK))


def solution(mesh):
    shape = dict(mesh.shape)

    def body(activations, output_grads, grad_factors, act_factors):
        kg, w = grad_factors.shape
        fits = (
            shape["groups"] == 2
            and shape["dp"] == 4
            and 4 <= shape["mp"] <= 7
            and w == 128
            and activations.shape[0] == SEQ_LEN
            and activations.shape[1] % 32 == 0
            and kg % (32 * PIECES) == 0
        )
        run = functools.partial(kernel_body, shape["mp"]) if fits else plain_body
        return run(activations, output_grads, grad_factors, act_factors)

    return jax.shard_map(
        body,
        mesh=mesh,
        in_specs=(
            P(("groups", "dp"), "mp"),
            P(("groups", "dp"), "mp"),
            P("mp", "dp"),
            P("mp", "dp"),
        ),
        out_specs=P(("groups", "dp"), None),
        check_vma=False,
    )
```
